1024 devices in a mesh: aux: 64 (over z, x), bas: 16 (over y, core).
Axes of the slice: x: 8, y: 8, z: 8, core: 2. Of those that a mesh axis runs over, the one named last changes fastest.
Arguments:
- three_centre: bfloat16 [16, 2, 64, 64, 8192], P('bas', None, None, None, 'aux'), may hold values from -0.25 to 0.25
- occ_green: bfloat16 [1024, 1024], P('bas'), may hold values from -0.5 to 0.5
- virt_blocks: bfloat16 [16, 64, 64], P('bas'), may hold values from -0.75 to 0.75
- row_lists: int32 [16, 2], P('bas'), may hold values from 0 to 15, as said below
Outputs:
- chi_band: float32 [8192, 2, 128], P('aux', None, 'bas')
The draws below stay inside these ranges and needn't reach their ends.
Inputs may be any that keep to these rules, and one draw needn't show every extreme that they name: `row_lists`: each row holds 2 different block numbers; the first is the row's own block number.
All inputs are finite; a program needn't handle non-finite values.
Results may differ from the reference program's by a relative error of at most 0.004.
Values may be sent and summed in bfloat16 or wider, within the bound.
No kernel may reach another device: no remote copies, remote signals or barrier semaphores. Data moves between devices by JAX's collectives and lax.ppermute only.
A program may use at most 32 MiB of HBM per device.

```python
import jax
import jax.numpy as jnp
from jax import lax

BB = 64
KB = 2
AUX_DEV = 128
NBLK = 16
NB = 1024
NAUX = 8192
N_AUX = 64


def draw_row_lists(key, part):
    key = jax.random.fold_in(key, 7)
    scores = jax.random.randint(key, (NBLK, NBLK), 0, 1 << 20) * NBLK + jnp.arange(NBLK, dtype=jnp.int32)[None, :]
    own = jnp.arange(NBLK, dtype=jnp.int32)
    scores = jnp.where(own[:, None] == own[None, :], -1, scores)
    order = jnp.argsort(scores, axis=1, stable=True)
    return order[:, :KB].astype(jnp.int32)


def shard_levels(stream_key, dims, split, smallest, top_value):
    factor_of, own = 1.0, jax.random.fold_in(stream_key, 6)
    for position, shards_of in split:
        steps = jnp.exp(jax.random.uniform(jax.random.fold_in(own, position), (shards_of,), jnp.float32, smallest / len(split), top_value / len(split)))
        factor_of = factor_of * jnp.repeat(steps, dims[position] // shards_of).reshape([-1 if axis == position else 1 for axis in range(len(dims))])
    return factor_of


def normal_values(key, extent, deviation, most, cuts=(), kind=jnp.bfloat16):
    drawn = jax.random.normal(key, extent, jnp.float32) * deviation
    if len(cuts) > 0:
        drawn = shard_levels(key, extent, cuts, -0.22, 0.18) * drawn
    return jnp.clip(drawn, min=-most, max=most).astype(kind)


def setup_inputs(seed: int = 0) -> dict:
    streams_of = jax.random.split(jax.random.key(seed), 5)
    return {
        "three_centre": normal_values(streams_of[0], (NBLK, KB, BB, BB, NAUX), (BB * 8) ** -0.5, 0.25, ((0, 16), (4, 64))),
        "occ_green": normal_values(streams_of[1], (NB, NB), (KB * BB) ** -0.5, 0.5, ((0, 16),)),
        "virt_blocks": normal_values(streams_of[2], (NBLK, BB, BB), BB ** -0.5, 0.75, ((0, 16),)),
        "row_lists": draw_row_lists(jax.random.fold_in(streams_of[4], 71), 0),
    }


def reference(three_centre, occ_green, virt_blocks, row_lists):
    nblk = row_lists.shape[0]
    kb = row_lists.shape[1]
    bb = virt_blocks.shape[1]
    naux = three_centre.shape[-1]
    grid = occ_green.reshape(nblk, bb, nblk, bb)
    zero_slab = jnp.zeros(three_centre.shape[:4] + (AUX_DEV,), three_centre.dtype)
    ahead_all = jnp.concatenate([three_centre[..., AUX_DEV:], zero_slab], axis=-1)

    def one_block(total, column):
        chosen = row_lists[column].astype(jnp.int32)
        sub = jnp.take(jnp.take(grid, chosen, axis=0), chosen, axis=2).reshape(kb * bb, kb * bb)
        slab = three_centre[column]
        half = jnp.dot(sub, slab.reshape(kb * bb, bb * naux), preferred_element_type=jnp.float32)
        half = half.astype(jnp.bfloat16).reshape(kb, bb, bb, naux)
        full = jnp.einsum("kvlp,ls->kvsp", half.astype(jnp.float32), virt_blocks[column].astype(jnp.float32))
        full = full.astype(jnp.bfloat16).astype(jnp.float32).reshape(-1, N_AUX, AUX_DEV)
        same = jnp.einsum("fap,faq->apq", full, slab.astype(jnp.float32).reshape(-1, N_AUX, AUX_DEV))
        ahead = jnp.einsum("fap,faq->apq", full, ahead_all[column].astype(jnp.float32).reshape(-1, N_AUX, AUX_DEV))
        return total + jnp.stack([same, ahead], axis=2), None

    start = jnp.zeros((N_AUX, AUX_DEV, 2, AUX_DEV), jnp.float32)
    total, unused = lax.scan(one_block, start, jnp.arange(nblk, dtype=jnp.int32))
    return total.reshape(naux, 2, AUX_DEV)
```

```python
import jax
import jax.numpy as jnp
from jax import lax
from jax.sharding import PartitionSpec as P


def shards(three_centre, occ_green, virt_blocks, row_lists):
    n_aux, n_bas = lax.axis_size("aux"), lax.axis_size("bas")
    me = lax.axis_index("bas")
    odd = lax.rem(me, 2) == 1
    first = jnp.logical_and(me == 0, lax.axis_index("aux") == 0)
    both = ("aux", "bas")
    bb = virt_blocks.shape[1]
    slab = three_centre[0]
    kb, aux_cols = slab.shape[0], slab.shape[-1]
    other_block = row_lists[0, 1]

    def at(a, c):
        return a * n_bas + c

    route = []
    for a in range(n_aux - 1):
        for c in range(n_bas):
            if c % 2 == 1:
                route.append((at(a, c), at(a + 1, c)))
            elif (a, c) == (0, 0):
                route.append((at(1, 0), at(0, 1)))
            else:
                route.append((at(a + 1, c), at(a, c)))
    arrived = lax.ppermute(slab, both, route)
    handed = lax.ppermute(arrived, both, [(at(0, 1), at(0, 0))])

    rows = occ_green.reshape(bb, n_bas, bb).transpose(1, 0, 2)
    own = lax.dynamic_index_in_dim(rows, me, 0, keepdims=False)
    beside = lax.dynamic_index_in_dim(rows, other_block, 0, keepdims=False)
    sent = jnp.stack([rows, jnp.broadcast_to(own, rows.shape)], axis=1)
    got = lax.all_to_all(sent, "bas", 0, 0)
    there = lax.dynamic_index_in_dim(got, other_block, 0, keepdims=False)
    matrix = jnp.concatenate(
        [jnp.concatenate([own, beside], axis=1), jnp.concatenate([there[0], there[1]], axis=1)], axis=0
    )
    virt = virt_blocks[0]
    matrix = jnp.where(odd, matrix.T, matrix)
    virt = jnp.where(odd, virt.T, virt)

    half = jnp.dot(matrix, slab.reshape(kb * bb, bb * aux_cols), preferred_element_type=jnp.float32)
    half = half.astype(jnp.bfloat16).reshape(kb, bb, bb, aux_cols)
    full = jnp.einsum("kvlp,ls->kvsp", half, virt, preferred_element_type=jnp.float32)
    flat_full = full.astype(jnp.bfloat16).reshape(-1, aux_cols)

    def tile(block):
        contract = (((0,), (0,)), ((), ()))
        product = lax.dot_general(
            block.reshape(-1, aux_cols), flat_full, contract, preferred_element_type=jnp.float32
        )
        return jnp.where(odd, product.T, product)

    same = tile(slab)
    pair = tile(jnp.where(first, handed, arrived))
    back = [(at(a + 1, c), at(a, c)) for a in range(n_aux - 1) for c in range(1, n_bas, 2)]
    returned = lax.ppermute(pair, both, back)
    ahead = jnp.where(odd, returned, pair)

    cut = aux_cols // n_bas
    parts = jnp.stack([same.reshape(n_bas, cut, aux_cols), ahead.reshape(n_bas, cut, aux_cols)], axis=1)
    total = lax.all_to_all(parts, "bas", 0, 0).sum(axis=0)
    return total.transpose(2, 0, 1)


def solution(mesh):
    in_specs = (
        P("bas", None, None, None, "aux"),
        P("bas", None),
        P("bas", None, None),
        P("bas", None),
    )
    out_specs = P("aux", None, "bas")
    return jax.shard_map(shards, mesh=mesh, in_specs=in_specs, out_specs=out_specs, check_vma=False)
```

```python
import jax
import jax.numpy as jnp
from jax import lax
from jax.experimental import pallas as pl
from jax.experimental.pallas import tpu as pltpu
from jax.sharding import PartitionSpec as P

VMEM = pl.BlockSpec(memory_space=pltpu.VMEM)
SMEM = pl.BlockSpec(memory_space=pltpu.SMEM)
ANY = pl.BlockSpec(memory_space=pl.ANY)
LIMIT = 24 * 2**20
PIECES = 4
GROUP = 4
STRIP = 16


def is_odd():
    return lax.rem(lax.axis_index("bas"), 2) == 1


def is_first():
    return jnp.logical_and(lax.axis_index("bas") == 0, lax.axis_index("aux") == 0)


def blocks_kernel(lists, occ, virt, slab, sent, upper, spread, held, sem):
    fetch = pltpu.make_async_copy(slab, held, sem)
    fetch.start()
    rows, width = occ.shape[0], 2 * occ.shape[0]
    low_lanes = lax.broadcasted_iota(jnp.int32, (rows, width), 1) < rows

    def in_high_lanes(number):
        tile = occ[:, pl.ds(pl.multiple_of(number // 2 * width, width), width)].astype(jnp.float32)
        return jnp.where(lax.rem(number, 2) == 1, tile, pltpu.roll(tile, rows, 1))

    own = in_high_lanes(lax.axis_index("bas"))
    upper[...] = jnp.where(low_lanes, pltpu.roll(own, rows, 1), in_high_lanes(lists[0, 1])).astype(upper.dtype)
    for t in range(occ.shape[1] // width):
        tile = occ[:, t * width : (t + 1) * width].astype(jnp.float32)
        sent[2 * t] = jnp.where(low_lanes, tile, own).astype(sent.dtype)
        sent[2 * t + 1] = jnp.where(low_lanes, pltpu.roll(tile, rows, 1), own).astype(sent.dtype)
    v = virt[0].astype(jnp.float32)
    v = jnp.where(is_odd(), v, v.T)
    zero = jnp.zeros_like(v)
    strips = [jnp.concatenate([v if i == j else zero for j in range(GROUP)], axis=1) for i in range(GROUP)]
    spread[...] = jnp.concatenate(strips, axis=0).astype(spread.dtype)
    fetch.wait()


def blocks_of(lists, occ, virt, slab):
    rows, cols = occ.shape
    return pl.pallas_call(
        blocks_kernel,
        out_shape=[
            jax.ShapeDtypeStruct((cols // rows, rows, 2 * rows), occ.dtype),
            jax.ShapeDtypeStruct((rows, 2 * rows), occ.dtype),
            jax.ShapeDtypeStruct((GROUP * rows, GROUP * rows), virt.dtype),
            jax.ShapeDtypeStruct(slab.shape, slab.dtype),
        ],
        in_specs=[SMEM, VMEM, VMEM, ANY],
        out_specs=[VMEM] * 4,
        scratch_shapes=[pltpu.SemaphoreType.DMA],
        compiler_params=pltpu.CompilerParams(vmem_limit_bytes=LIMIT),
    )(lists, occ, virt, slab)


def transform_kernel(lists, upper, got, spread, slab, left, same, halves):
    n_rows, bb, cols = slab.shape
    matrix = jnp.concatenate([upper[...], got[lists[0, 1]]], axis=0).astype(jnp.float32)
    matrix = jnp.where(is_odd(), matrix.T, matrix).astype(jnp.bfloat16)
    for r in range(0, bb, STRIP):
        turned = jnp.swapaxes(slab[:, r : r + STRIP, :], 0, 1)
        parts = []
        for q in range(0, STRIP, 2):
            two = jnp.concatenate([turned[q], turned[q + 1]], axis=1)
            half = jnp.dot(matrix, two, preferred_element_type=jnp.float32).astype(jnp.bfloat16)
            parts += [half[:, :cols], half[:, cols:]]
        halves[:, r : r + STRIP, :] = jnp.swapaxes(jnp.stack(parts), 0, 1)
    for g in range(0, n_rows, GROUP):
        half = halves[g : g + GROUP].reshape(GROUP * bb, cols)
        full = jnp.dot(spread[...], half, preferred_element_type=jnp.float32)
        left[:, g * bb : (g + GROUP) * bb] = full.T.astype(jnp.bfloat16)
    store_product(same, left, slab.reshape(n_rows * bb, cols))


def store_product(out, left, right):
    depth = left.shape[1]
    step = depth // PIECES
    total = jnp.zeros(out.shape, jnp.float32)
    for i in range(0, depth, step):
        total += jnp.dot(left[:, i : i + step], right[i : i + step], preferred_element_type=jnp.float32)
    out[...] = jnp.where(is_odd(), total, total.T)


def transform(lists, upper, got, spread, slab):
    n_rows, bb, cols = slab.shape
    return pl.pallas_call(
        transform_kernel,
        out_shape=[
            jax.ShapeDtypeStruct((cols, n_rows * bb), jnp.bfloat16),
            jax.ShapeDtypeStruct((cols, cols), jnp.float32),
        ],
        in_specs=[SMEM] + [VMEM] * 4,
        out_specs=[VMEM, VMEM],
        scratch_shapes=[pltpu.VMEM(slab.shape, slab.dtype)],
        compiler_params=pltpu.CompilerParams(vmem_limit_bytes=LIMIT),
    )(lists, upper, got, spread, slab)


def pair_kernel(left, arrived, handed, out, block, sem):
    @pl.when(is_first())
    def _():
        copy = pltpu.make_async_copy(handed, block, sem)
        copy.start()
        copy.wait()
        store_product(out, left, block)

    @pl.when(jnp.logical_not(is_first()))
    def _():
        store_product(out, left, arrived)


def pair_product(left, arrived, handed):
    cols = arrived.shape[1]
    return pl.pallas_call(
        pair_kernel,
        out_shape=jax.ShapeDtypeStruct((cols, cols), jnp.float32),
        in_specs=[VMEM, VMEM, ANY],
        out_specs=VMEM,
        scratch_shapes=[pltpu.VMEM(arrived.shape, arrived.dtype), pltpu.SemaphoreType.DMA],
        compiler_params=pltpu.CompilerParams(vmem_limit_bytes=LIMIT),
    )(left, arrived, handed)


def shards(three_centre, occ_green, virt_blocks, row_lists):
    n_aux, n_bas = lax.axis_size("aux"), lax.axis_size("bas")
    both = ("aux", "bas")
    bb = virt_blocks.shape[1]
    slab = three_centre[0]
    kb, aux_cols = slab.shape[0], slab.shape[-1]

    def at(a, c):
        return a * n_bas + c

    route = []
    for a in range(n_aux - 1):
        for c in range(n_bas):
            if c % 2 == 1:
                route.append((at(a, c), at(a + 1, c)))
            elif (a, c) == (0, 0):
                route.append((at(1, 0), at(0, 1)))
            else:
                route.append((at(a + 1, c), at(a, c)))
    arrived = lax.ppermute(slab, both, route)

    sent, upper, spread, held = blocks_of(row_lists, occ_green, virt_blocks, slab.reshape(kb * bb, bb, aux_cols))
    got = lax.all_to_all(sent, "bas", 0, 0)
    left, same = transform(row_lists, upper, got, spread, held)

    arrived, left, same = lax.optimization_barrier((arrived, left, same))
    handed = lax.ppermute(arrived, both, [(at(0, 1), at(0, 0))])
    pair = pair_product(left, arrived.reshape(-1, aux_cols), handed.reshape(-1, aux_cols))
    back = [(at(a + 1, c), at(a, c)) for a in range(n_aux - 1) for c in range(1, n_bas, 2)]
    returned = lax.ppermute(pair, both, back)
    ahead = jnp.where(is_odd(), returned, pair)

    cut = aux_cols // n_bas
    parts = jnp.stack([same.reshape(n_bas, cut, aux_cols), ahead.reshape(n_bas, cut, aux_cols)], axis=1)
    total = lax.all_to_all(parts, "bas", 0, 0).sum(axis=0)
    return total.transpose(2, 0, 1)


def solution(mesh):
    in_specs = (
        P("bas", None, None, None, "aux"),
        P("bas", None),
        P("bas", None, None),
        P("bas", None),
    )
    out_specs = P("aux", None, "bas")
    return jax.shard_map(shards, mesh=mesh, in_specs=in_specs, out_specs=out_specs, check_vma=False)
```

```python
import jax
import jax.numpy as jnp
from jax import lax
from jax.experimental import pallas as pl
from jax.experimental.pallas import tpu as pltpu
from jax.sharding import PartitionSpec as P

VMEM = pl.BlockSpec(memory_space=pltpu.VMEM)
SMEM = pl.BlockSpec(memory_space=pltpu.SMEM)
HBM = pl.BlockSpec(memory_space=pltpu.HBM)
LIMIT = 24 * 2**20
PIECES = 4
GROUP = 4
STRIP = 16


def is_odd():
    return lax.rem(lax.axis_index("bas"), 2) == 1


def blocks_kernel(lists_hbm, occ_hbm, virt_hbm, slab, sent, upper, spread, held, lists, occ, virt, sems):
    fetches = [
        pltpu.make_async_copy(lists_hbm, lists, sems.at[0]),
        pltpu.make_async_copy(occ_hbm, occ, sems.at[1]),
        pltpu.make_async_copy(virt_hbm, virt, sems.at[2]),
        pltpu.make_async_copy(slab, held, sems.at[3]),
    ]
    for fetch in fetches:
        fetch.start()
    fetches[0].wait()
    fetches[1].wait()
    rows, width = occ.shape[0], 2 * occ.shape[0]
    low_lanes = lax.broadcasted_iota(jnp.int32, (rows, width), 1) < rows

    def in_high_lanes(number):
        tile = occ[:, pl.ds(pl.multiple_of(number // 2 * width, width), width)].astype(jnp.float32)
        return jnp.where(lax.rem(number, 2) == 1, tile, pltpu.roll(tile, rows, 1))

    own = in_high_lanes(lax.axis_index("bas"))
    upper[...] = jnp.where(low_lanes, pltpu.roll(own, rows, 1), in_high_lanes(lists[0, 1])).astype(upper.dtype)
    for t in range(occ.shape[1] // width):
        tile = occ[:, t * width : (t + 1) * width].astype(jnp.float32)
        sent[2 * t] = jnp.where(low_lanes, tile, own).astype(sent.dtype)
        sent[2 * t + 1] = jnp.where(low_lanes, pltpu.roll(tile, rows, 1), own).astype(sent.dtype)
    fetches[2].wait()
    v = virt[0].astype(jnp.float32)
    v = jnp.where(is_odd(), v, v.T)
    zero = jnp.zeros_like(v)
    strips = [jnp.concatenate([v if i == j else zero for j in range(GROUP)], axis=1) for i in range(GROUP)]
    spread[...] = jnp.concatenate(strips, axis=0).astype(spread.dtype)
    fetches[3].wait()


def blocks_of(lists, occ, virt, slab):
    rows, cols = occ.shape
    return pl.pallas_call(
        blocks_kernel,
        out_shape=[
            jax.ShapeDtypeStruct((cols // rows, rows, 2 * rows), occ.dtype),
            jax.ShapeDtypeStruct((rows, 2 * rows), occ.dtype),
            jax.ShapeDtypeStruct((GROUP * rows, GROUP * rows), virt.dtype),
            jax.ShapeDtypeStruct(slab.shape, slab.dtype),
        ],
        in_specs=[HBM] * 4,
        out_specs=[VMEM] * 4,
        scratch_shapes=[
            pltpu.SMEM(lists.shape, lists.dtype),
            pltpu.VMEM(occ.shape, occ.dtype),
            pltpu.VMEM(virt.shape, virt.dtype),
            pltpu.SemaphoreType.DMA((4,)),
        ],
        compiler_params=pltpu.CompilerParams(vmem_limit_bytes=LIMIT),
    )(*[pltpu.with_memory_space_constraint(x, pltpu.HBM) for x in (lists, occ, virt, slab)])


def transform_kernel(lists, upper, got, spread, slab, left, same, halves):
    n_rows, bb, cols = slab.shape
    matrix = jnp.concatenate([upper[...], got[lists[0, 1]]], axis=0).astype(jnp.float32)
    matrix = jnp.where(is_odd(), matrix.T, matrix).astype(jnp.bfloat16)
    for r in range(0, bb, STRIP):
        turned = jnp.swapaxes(slab[:, r : r + STRIP, :], 0, 1)
        parts = []
        for q in range(0, STRIP, 2):
            two = jnp.concatenate([turned[q], turned[q + 1]], axis=1)
            half = jnp.dot(matrix, two, preferred_element_type=jnp.float32).astype(jnp.bfloat16)
            parts += [half[:, :cols], half[:, cols:]]
        halves[:, r : r + STRIP, :] = jnp.swapaxes(jnp.stack(parts), 0, 1)
    for g in range(0, n_rows, GROUP):
        half = halves[g : g + GROUP].reshape(GROUP * bb, cols)
        full = jnp.dot(spread[...], half, preferred_element_type=jnp.float32)
        left[:, g * bb : (g + GROUP) * bb] = full.T.astype(jnp.bfloat16)
    store_product(same, left, slab.reshape(n_rows * bb, cols))


def store_product(out, left, right):
    depth = left.shape[1]
    step = depth // PIECES
    total = jnp.zeros(out.shape, jnp.float32)
    for i in range(0, depth, step):
        total += jnp.dot(left[:, i : i + step], right[i : i + step], preferred_element_type=jnp.float32)
    out[...] = jnp.where(is_odd(), total, total.T)


def transform(lists, upper, got, spread, slab):
    n_rows, bb, cols = slab.shape
    return pl.pallas_call(
        transform_kernel,
        out_shape=[
            jax.ShapeDtypeStruct((cols, n_rows * bb), jnp.bfloat16),
            jax.ShapeDtypeStruct((cols, cols), jnp.float32),
        ],
        in_specs=[SMEM] + [VMEM] * 4,
        out_specs=[VMEM, VMEM],
        scratch_shapes=[pltpu.VMEM(slab.shape, slab.dtype)],
        compiler_params=pltpu.CompilerParams(vmem_limit_bytes=LIMIT),
    )(lists, upper, got, spread, slab)


def pair_kernel(left, arrived, out):
    store_product(out, left, arrived)


def pair_product(left, arrived):
    cols = arrived.shape[1]
    return pl.pallas_call(
        pair_kernel,
        out_shape=jax.ShapeDtypeStruct((cols, cols), jnp.float32),
        in_specs=[VMEM, VMEM],
        out_specs=VMEM,
        compiler_params=pltpu.CompilerParams(vmem_limit_bytes=LIMIT),
    )(left, arrived)


def shards(three_centre, occ_green, virt_blocks, row_lists):
    n_aux, n_bas = lax.axis_size("aux"), lax.axis_size("bas")
    both = ("aux", "bas")
    bb = virt_blocks.shape[1]
    slab = three_centre[0]
    kb, aux_cols = slab.shape[0], slab.shape[-1]

    def at(a, c):
        return a * n_bas + c

    route = []
    for a in range(n_aux - 1):
        for c in range(n_bas):
            if c % 2 == 1:
                route.append((at(a, c), at(a + 1, c)))
            else:
                route.append((at(a + 1, c), at(a, c)))
    arrived = lax.ppermute(slab, both, route)

    sent, upper, spread, held = blocks_of(row_lists, occ_green, virt_blocks, slab.reshape(kb * bb, bb, aux_cols))
    got = lax.all_to_all(sent, "bas", 0, 0)
    left, same = transform(row_lists, upper, got, spread, held)

    arrived, left, same = lax.optimization_barrier((arrived, left, same))
    pair = pair_product(left, arrived.reshape(-1, aux_cols))
    back = [(at(a + 1, c), at(a, c)) for a in range(n_aux - 1) for c in range(1, n_bas, 2)]
    returned = lax.ppermute(pair, both, back)
    ahead = jnp.where(is_odd(), returned, pair)

    cut = aux_cols // n_bas
    parts = jnp.stack([same.reshape(n_bas, cut, aux_cols), ahead.reshape(n_bas, cut, aux_cols)], axis=1)
    total = lax.all_to_all(parts, "bas", 0, 0).sum(axis=0)
    return total.transpose(2, 0, 1)


def solution(mesh):
    in_specs = (
        P("bas", None, None, None, "aux"),
        P("bas", None),
        P("bas", None, None),
        P("bas", None),
    )
    out_specs = P("aux", None, "bas")
    return jax.shard_map(shards, mesh=mesh, in_specs=in_specs, out_specs=out_specs, check_vma=False)
```

```python
import jax
import jax.numpy as jnp
from jax import lax
from jax.experimental import pallas as pl
from jax.experimental.pallas import tpu as pltpu
from jax.sharding import PartitionSpec as P

VMEM = pl.BlockSpec(memory_space=pltpu.VMEM)
SMEM = pl.BlockSpec(memory_space=pltpu.SMEM)
HBM = pl.BlockSpec(memory_space=pltpu.HBM)
LIMIT = 24 * 2**20
PIECES = 4
GROUP = 4
STRIP = 16


def is_odd():
    return lax.rem(lax.axis_index("bas"), 2) == 1


def blocks_kernel(lists_hbm, occ_hbm, virt_hbm, slab, sent, upper, spread, held, lists, occ, virt, sems):
    fetches = [
        pltpu.make_async_copy(lists_hbm, lists, sems.at[0]),
        pltpu.make_async_copy(occ_hbm, occ, sems.at[1]),
        pltpu.make_async_copy(virt_hbm, virt, sems.at[2]),
        pltpu.make_async_copy(slab, held, sems.at[3]),
    ]
    for fetch in fetches:
        fetch.start()
    fetches[0].wait()
    fetches[1].wait()
    rows, width = occ.shape[0], 2 * occ.shape[0]
    low_lanes = lax.broadcasted_iota(jnp.int32, (rows, width), 1) < rows

    def in_high_lanes(number):
        tile = occ[:, pl.ds(pl.multiple_of(number // 2 * width, width), width)].astype(jnp.float32)
        return jnp.where(lax.rem(number, 2) == 1, tile, pltpu.roll(tile, rows, 1))

    own = in_high_lanes(lax.axis_index("bas"))
    upper[...] = jnp.where(low_lanes, pltpu.roll(own, rows, 1), in_high_lanes(lists[0, 1])).astype(upper.dtype)
    for t in range(occ.shape[1] // width):
        tile = occ[:, t * width : (t + 1) * width].astype(jnp.float32)
        sent[2 * t] = jnp.where(low_lanes, tile, own).astype(sent.dtype)
        sent[2 * t + 1] = jnp.where(low_lanes, pltpu.roll(tile, rows, 1), own).astype(sent.dtype)
    fetches[2].wait()
    v = virt[0].astype(jnp.float32)
    v = jnp.where(is_odd(), v, v.T)
    zero = jnp.zeros_like(v)
    strips = [jnp.concatenate([v if i == j else zero for j in range(GROUP)], axis=1) for i in range(GROUP)]
    spread[...] = jnp.concatenate(strips, axis=0).astype(spread.dtype)
    fetches[3].wait()


def blocks_of(lists, occ, virt, slab):
    rows, cols = occ.shape
    return pl.pallas_call(
        blocks_kernel,
        out_shape=[
            jax.ShapeDtypeStruct((cols // rows, rows, 2 * rows), occ.dtype),
            jax.ShapeDtypeStruct((rows, 2 * rows), occ.dtype),
            jax.ShapeDtypeStruct((GROUP * rows, GROUP * rows), virt.dtype),
            jax.ShapeDtypeStruct(slab.shape, slab.dtype),
        ],
        in_specs=[HBM] * 4,
        out_specs=[VMEM] * 4,
        scratch_shapes=[
            pltpu.SMEM(lists.shape, lists.dtype),
            pltpu.VMEM(occ.shape, occ.dtype),
            pltpu.VMEM(virt.shape, virt.dtype),
            pltpu.SemaphoreType.DMA((4,)),
        ],
        compiler_params=pltpu.CompilerParams(vmem_limit_bytes=LIMIT),
    )(*[pltpu.with_memory_space_constraint(x, pltpu.HBM) for x in (lists, occ, virt, slab)])


def transform_kernel(lists, upper, got, spread, slab, left, same, halves):
    n_rows, bb, cols = slab.shape
    matrix = jnp.concatenate([upper[...], got[lists[0, 1]]], axis=0).astype(jnp.float32)
    matrix = jnp.where(is_odd(), matrix.T, matrix).astype(jnp.bfloat16)
    for r in range(0, bb, STRIP):
        turned = jnp.swapaxes(slab[:, r : r + STRIP, :], 0, 1)
        parts = []
        for q in range(0, STRIP, 2):
            two = jnp.concatenate([turned[q], turned[q + 1]], axis=1)
            half = jnp.dot(matrix, two, preferred_element_type=jnp.float32).astype(jnp.bfloat16)
            parts += [half[:, :cols], half[:, cols:]]
        halves[:, r : r + STRIP, :] = jnp.swapaxes(jnp.stack(parts), 0, 1)
    for g in range(0, n_rows, GROUP):
        half = halves[g : g + GROUP].reshape(GROUP * bb, cols)
        full = jnp.dot(spread[...], half, preferred_element_type=jnp.float32)
        left[:, g * bb : (g + GROUP) * bb] = full.T.astype(jnp.bfloat16)
    store_product(same, left, slab.reshape(n_rows * bb, cols))


def store_product(out, left, right):
    depth = left.shape[1]
    step = depth // PIECES
    total = jnp.zeros(out.shape, jnp.float32)
    for i in range(0, depth, step):
        total += jnp.dot(left[:, i : i + step], right[i : i + step], preferred_element_type=jnp.float32)
    out[...] = jnp.where(is_odd(), total, total.T)


def transform(lists, upper, got, spread, slab):
    n_rows, bb, cols = slab.shape
    return pl.pallas_call(
        transform_kernel,
        out_shape=[
            jax.ShapeDtypeStruct((cols, n_rows * bb), jnp.bfloat16),
            jax.ShapeDtypeStruct((cols, cols), jnp.float32),
        ],
        in_specs=[SMEM] + [VMEM] * 4,
        out_specs=[VMEM, VMEM],
        scratch_shapes=[pltpu.VMEM(slab.shape, slab.dtype)],
        compiler_params=pltpu.CompilerParams(vmem_limit_bytes=LIMIT),
    )(lists, upper, got, spread, slab)


def pair_kernel(left, *refs):
    *arrived, out = refs
    depth = arrived[0].shape[0]
    step = depth // 2
    total = jnp.zeros(out.shape, jnp.float32)
    for k, block in enumerate(arrived):
        for i in range(0, depth, step):
            span = left[:, k * depth + i : k * depth + i + step]
            total += jnp.dot(span, block[i : i + step], preferred_element_type=jnp.float32)
    out[...] = jnp.where(is_odd(), total, total.T)


def pair_product(left, arrived):
    cols = arrived[0].shape[1]
    return pl.pallas_call(
        pair_kernel,
        out_shape=jax.ShapeDtypeStruct((cols, cols), jnp.float32),
        in_specs=[VMEM] * (1 + len(arrived)),
        out_specs=VMEM,
        compiler_params=pltpu.CompilerParams(vmem_limit_bytes=LIMIT),
    )(left, *arrived)


def shards(three_centre, occ_green, virt_blocks, row_lists):
    n_aux, n_bas = lax.axis_size("aux"), lax.axis_size("bas")
    both = ("aux", "bas")
    bb = virt_blocks.shape[1]
    slab = three_centre[0]
    kb, aux_cols = slab.shape[0], slab.shape[-1]

    def at(a, c):
        return a * n_bas + c

    route = []
    for a in range(n_aux - 1):
        for c in range(n_bas):
            if c % 2 == 1:
                route.append((at(a, c), at(a + 1, c)))
            else:
                route.append((at(a + 1, c), at(a, c)))
    arrived = [lax.ppermute(slab[k], both, route) for k in range(kb)]

    sent, upper, spread, held = blocks_of(row_lists, occ_green, virt_blocks, slab.reshape(kb * bb, bb, aux_cols))
    got = lax.all_to_all(sent, "bas", 0, 0)
    left, same = transform(row_lists, upper, got, spread, held)

    arrived, left, same = lax.optimization_barrier((arrived, left, same))
    pair = pair_product(left, [block.reshape(-1, aux_cols) for block in arrived])
    back = [(at(a + 1, c), at(a, c)) for a in range(n_aux - 1) for c in range(1, n_bas, 2)]
    returned = lax.ppermute(pair, both, back)
    ahead = jnp.where(is_odd(), returned, pair)

    cut = aux_cols // n_bas
    parts = jnp.stack([same.reshape(n_bas, cut, aux_cols), ahead.reshape(n_bas, cut, aux_cols)], axis=1)
    total = lax.all_to_all(parts, "bas", 0, 0).sum(axis=0)
    return total.transpose(2, 0, 1)


def solution(mesh):
    in_specs = (
        P("bas", None, None, None, "aux"),
        P("bas", None),
        P("bas", None, None),
        P("bas", None),
    )
    out_specs = P("aux", None, "bas")
    return jax.shard_map(shards, mesh=mesh, in_specs=in_specs, out_specs=out_specs, check_vma=False)
```

```python
import jax
import jax.numpy as jnp
from jax import lax
from jax.experimental import pallas as pl
from jax.experimental.pallas import tpu as pltpu
from jax.sharding import PartitionSpec as P

VMEM = pl.BlockSpec(memory_space=pltpu.VMEM)
SMEM = pl.BlockSpec(memory_space=pltpu.SMEM)
HBM = pl.BlockSpec(memory_space=pltpu.HBM)
LIMIT = 24 * 2**20
PIECES = 4
GROUP = 4
STRIP = 16


def is_odd():
    return lax.rem(lax.axis_index("bas"), 2) == 1


def blocks_kernel(lists_hbm, occ_hbm, virt_hbm, slab, sent, upper, spread, held, lists, occ, virt, sems):
    fetches = [
        pltpu.make_async_copy(lists_hbm, lists, sems.at[0]),
        pltpu.make_async_copy(occ_hbm, occ, sems.at[1]),
        pltpu.make_async_copy(virt_hbm, virt, sems.at[2]),
        pltpu.make_async_copy(slab, held, sems.at[3]),
    ]
    for fetch in fetches:
        fetch.start()
    fetches[0].wait()
    fetches[1].wait()
    rows, width = occ.shape[0], 2 * occ.shape[0]
    low_lanes = lax.broadcasted_iota(jnp.int32, (rows, width), 1) < rows

    def in_high_lanes(number):
        tile = occ[:, pl.ds(pl.multiple_of(number // 2 * width, width), width)].astype(jnp.float32)
        return jnp.where(lax.rem(number, 2) == 1, tile, pltpu.roll(tile, rows, 1))

    own = in_high_lanes(lax.axis_index("bas"))
    upper[...] = jnp.where(low_lanes, pltpu.roll(own, rows, 1), in_high_lanes(lists[0, 1])).astype(upper.dtype)
    for t in range(occ.shape[1] // width):
        tile = occ[:, t * width : (t + 1) * width].astype(jnp.float32)
        sent[2 * t] = jnp.where(low_lanes, tile, own).astype(sent.dtype)
        sent[2 * t + 1] = jnp.where(low_lanes, pltpu.roll(tile, rows, 1), own).astype(sent.dtype)
    fetches[2].wait()
    v = virt[0].astype(jnp.float32)
    v = jnp.where(is_odd(), v, v.T)
    zero = jnp.zeros_like(v)
    strips = [jnp.concatenate([v if i == j else zero for j in range(GROUP)], axis=1) for i in range(GROUP)]
    spread[...] = jnp.concatenate(strips, axis=0).astype(spread.dtype)
    fetches[3].wait()


def blocks_of(lists, occ, virt, slab):
    rows, cols = occ.shape
    return pl.pallas_call(
        blocks_kernel,
        out_shape=[
            jax.ShapeDtypeStruct((cols // rows, rows, 2 * rows), occ.dtype),
            jax.ShapeDtypeStruct((rows, 2 * rows), occ.dtype),
            jax.ShapeDtypeStruct((GROUP * rows, GROUP * rows), virt.dtype),
            jax.ShapeDtypeStruct(slab.shape, slab.dtype),
        ],
        in_specs=[HBM] * 4,
        out_specs=[VMEM] * 4,
        scratch_shapes=[
            pltpu.SMEM(lists.shape, lists.dtype),
            pltpu.VMEM(occ.shape, occ.dtype),
            pltpu.VMEM(virt.shape, virt.dtype),
            pltpu.SemaphoreType.DMA((4,)),
        ],
        compiler_params=pltpu.CompilerParams(vmem_limit_bytes=LIMIT),
    )(*[pltpu.with_memory_space_constraint(x, pltpu.HBM) for x in (lists, occ, virt, slab)])


def transform_kernel(lists, upper, got, spread, slab, left, same, halves):
    n_rows, bb, cols = slab.shape
    matrix = jnp.concatenate([upper[...], got[lists[0, 1]]], axis=0).astype(jnp.float32)
    matrix = jnp.where(is_odd(), matrix.T, matrix).astype(jnp.bfloat16)
    for r in range(0, bb, STRIP):
        turned = jnp.swapaxes(slab[:, r : r + STRIP, :], 0, 1)
        parts = []
        for q in range(0, STRIP, 2):
            two = jnp.concatenate([turned[q], turned[q + 1]], axis=1)
            half = jnp.dot(matrix, two, preferred_element_type=jnp.float32).astype(jnp.bfloat16)
            parts += [half[:, :cols], half[:, cols:]]
        halves[:, r : r + STRIP, :] = jnp.swapaxes(jnp.stack(parts), 0, 1)
    for g in range(0, n_rows, GROUP):
        half = halves[g : g + GROUP].reshape(GROUP * bb, cols)
        full = jnp.dot(spread[...], half, preferred_element_type=jnp.float32)
        left[:, g * bb : (g + GROUP) * bb] = full.T.astype(jnp.bfloat16)
    store_product(same, left, slab.reshape(n_rows * bb, cols))


def store_product(out, left, right):
    depth = left.shape[1]
    step = depth // PIECES
    total = jnp.zeros(out.shape, jnp.float32)
    for i in range(0, depth, step):
        total += jnp.dot(left[:, i : i + step], right[i : i + step], preferred_element_type=jnp.float32)
    out[...] = jnp.where(is_odd(), total, total.T)


def transform(lists, upper, got, spread, slab):
    n_rows, bb, cols = slab.shape
    return pl.pallas_call(
        transform_kernel,
        out_shape=[
            jax.ShapeDtypeStruct((cols, n_rows * bb), jnp.bfloat16),
            jax.ShapeDtypeStruct((cols, cols), jnp.float32),
        ],
        in_specs=[SMEM] + [VMEM] * 4,
        out_specs=[VMEM, VMEM],
        scratch_shapes=[pltpu.VMEM(slab.shape, slab.dtype)],
        compiler_params=pltpu.CompilerParams(vmem_limit_bytes=LIMIT),
    )(lists, upper, got, spread, slab)


def pair_kernel(left, arrived, out):
    store_product(out, left, arrived)


def pair_product(left, arrived):
    cols = arrived.shape[1]
    return pl.pallas_call(
        pair_kernel,
        out_shape=jax.ShapeDtypeStruct((cols, cols), jnp.float32),
        in_specs=[VMEM, VMEM],
        out_specs=VMEM,
        compiler_params=pltpu.CompilerParams(vmem_limit_bytes=LIMIT),
    )(left, arrived)


def shards(three_centre, occ_green, virt_blocks, row_lists):
    n_aux, n_bas = lax.axis_size("aux"), lax.axis_size("bas")
    both = ("aux", "bas")
    bb = virt_blocks.shape[1]
    slab = three_centre[0]
    kb, aux_cols = slab.shape[0], slab.shape[-1]

    def at(a, c):
        return a * n_bas + c

    route = []
    for a in range(n_aux - 1):
        for c in range(n_bas):
            if c % 2 == 1:
                route.append((at(a, c), at(a + 1, c)))
            else:
                route.append((at(a + 1, c), at(a, c)))
    arrived = lax.ppermute(slab, both, route)

    sent, upper, spread, held = blocks_of(row_lists, occ_green, virt_blocks, slab.reshape(kb * bb, bb, aux_cols))
    got = lax.all_to_all(sent, "bas", 0, 0)
    left, same = transform(row_lists, upper, got, spread, held)

    arrived, left, same = lax.optimization_barrier((arrived, left, same))
    pair = pair_product(left, arrived.reshape(-1, aux_cols))
    back = [(at(a + 1, c), at(a, c)) for a in range(n_aux - 1) for c in range(1, n_bas, 2)]
    returned = lax.ppermute(pair, both, back)
    ahead = jnp.where(is_odd(), returned, pair)

    cut = aux_cols // n_bas
    parts = jnp.stack([same.reshape(n_bas, cut, aux_cols), ahead.reshape(n_bas, cut, aux_cols)], axis=1)
    parts = parts.reshape(n_bas, 2 * cut, aux_cols).astype(jnp.bfloat16)
    total = lax.all_to_all(parts, "bas", 0, 0).astype(jnp.float32).sum(axis=0).reshape(2, cut, aux_cols)
    return total.transpose(2, 0, 1)


def solution(mesh):
    in_specs = (
        P("bas", None, None, None, "aux"),
        P("bas", None),
        P("bas", None, None),
        P("bas", None),
    )
    out_specs = P("aux", None, "bas")
    return jax.shard_map(shards, mesh=mesh, in_specs=in_specs, out_specs=out_specs, check_vma=False)
```
